32 devices in a mesh: parts: 2 (over x), ctx: 16 (over z, y, core).
Axes of the slice: x: 2, y: 2, z: 4, core: 2. Of those that a mesh axis runs over, the one named last changes fastest.
Arguments:
- query_rows: bfloat16 [2, 4096, 1536], P(None, ('parts', 'ctx')), parts along dimension 1, may hold values from -6 to 6
- key_rows: bfloat16 [2, 4096, 1536], P(None, ('parts', 'ctx')), parts along dimension 1, may hold values from -4 to 4
- value_rows: bfloat16 [2, 4096, 1536], P(None, ('parts', 'ctx')), parts along dimension 1, may hold values from -12 to 12
- step_rates: float32 [2, 4096, 4], P(None, ('parts', 'ctx')), parts along dimension 1, may hold values from 0.01 to 1
- gate_weight: float32 [3072, 384], P(('parts', 'ctx')), parts along dimension 0, may hold values from -0.3125 to 0.3125
- up_weight: float32 [3072, 384], P(('parts', 'ctx')), parts along dimension 0, may hold values from -0.3125 to 0.3125
- down_weight: float32 [3072, 384], P(('parts', 'ctx')), parts along dimension 0, may hold values from -0.3125 to 0.3125
Outputs:
- attended: bfloat16 [2, 4096, 1536], P(None, ('parts', 'ctx')), parts along dimension 1
- gate_next: float32 [3072, 384], P(('parts', 'ctx')), parts along dimension 0
- up_next: float32 [3072, 384], P(('parts', 'ctx')), parts along dimension 0
- down_next: float32 [3072, 384], P(('parts', 'ctx')), parts along dimension 0
The draws below stay inside these ranges and needn't reach their ends.
There are 2 independent parts, one for each index of `parts`. The reference program is written for one: setup_inputs(seed, part) draws one part's arguments, and reference() takes and returns one part's arrays. A program takes and returns all parts, laid end to end along the dimension named above; each array names one. Nothing has to cross between parts.
All inputs are finite; a program needn't handle non-finite values.
Results may differ from the reference program's by a relative error of at most 0.0081.
Values may be sent and summed in bfloat16 or wider, within the bound.
A program may use at most 64 MiB of HBM per device.

```python
import math
import jax
import jax.numpy as jnp
from jax import lax

H = 4
DH = 384
FH = 384
SPANS = 2
TOK_DEV = 128
TOKENS = 2048
HD = 1536
HF = 1536


def token_fields(key):
    shape = (SPANS, TOKENS, HD)
    key_base = jax.random.fold_in(key, 101)
    value_base = jax.random.fold_in(key, 202)
    pairing_base = jax.random.fold_in(key, 404)
    key_noise = jax.random.truncated_normal(key_base, -4.0, 4.0, shape, jnp.float32)
    value_noise = jax.random.truncated_normal(value_base, -4.0, 4.0, shape, jnp.float32)
    blocks = TOKENS // TOK_DEV
    pairing = jax.random.permutation(pairing_base, blocks)
    token_block = jnp.arange(TOKENS, dtype=jnp.int32) // TOK_DEV
    feature_block = jnp.arange(HD, dtype=jnp.int32) // (HD // blocks)
    boosted = jnp.where(pairing[token_block][:, None] == feature_block[None, :], 5.0, 1.0).astype(jnp.float32)
    keys_drawn = key_noise
    values_drawn = 0.9 * key_noise + 0.44 * boosted[None, :, :] * value_noise
    return (keys_drawn, jnp.clip(values_drawn, -12.0, 12.0))


def draw_key_rows(key, part):
    return token_fields(key)[0].astype(jnp.bfloat16)


def draw_value_rows(key, part):
    return token_fields(key)[1].astype(jnp.bfloat16)


def level_of(own_key, extent, cuts, smallest, largest):
    factor_of = 1.0
    for axis_at, parts in cuts:
        heights = jax.random.uniform(jax.random.fold_in(jax.random.fold_in(own_key, 6), axis_at), (parts,), jnp.float32, smallest / len(cuts), largest / len(cuts))
        factor_of = factor_of * jnp.repeat(jnp.exp(heights), extent[axis_at] // parts).reshape((-1,) + (1,) * (len(extent) - 1 - axis_at))
    return factor_of


def noise(own_key, dims, spread, limit, shards=(), kind=jnp.bfloat16):
    factor_of = level_of(own_key, dims, shards, -0.22, 0.18) if shards else 1.0
    result = jax.random.normal(own_key, dims, jnp.float32) * spread * factor_of
    return jnp.minimum(jnp.maximum(result, -limit), limit).astype(kind)


def setup_inputs(seed: int = 0, part: int = 0) -> dict:
    seeds = jax.random.split(jax.random.key(seed), 8)
    own_keys = jax.random.split(jax.random.fold_in(seeds[7], part), 8)
    query_rows = noise(own_keys[0], (SPANS, TOKENS, HD), 1.0, 6.0, ((1, 16),))
    key_rows = draw_key_rows(jax.random.fold_in(jax.random.fold_in(seeds[7], part), 71), part)
    value_rows = draw_value_rows(jax.random.fold_in(jax.random.fold_in(seeds[7], part), 71), part)
    step_rates = jnp.clip(jnp.exp(math.log(1.0) - 4.6051702 * jax.random.uniform(own_keys[3], (SPANS, TOKENS, H), jnp.float32) ** level_of(own_keys[3], (SPANS, TOKENS, H), ((1, 16),), -0.2, 0.2)), 0.01, 1.0)
    gate_weight = noise(own_keys[4], (HF, DH), DH ** -0.5, 0.3125, ((0, 16),), jnp.float32)
    up_weight = noise(own_keys[5], (HF, DH), DH ** -0.5, 0.3125, ((0, 16),), jnp.float32)
    down_weight = noise(own_keys[6], (HD, FH), FH ** -0.5, 0.3125, ((0, 16),), jnp.float32)
    return {"query_rows": query_rows, "key_rows": key_rows, "value_rows": value_rows, "step_rates": step_rates, "gate_weight": gate_weight, "up_weight": up_weight, "down_weight": down_weight}


def silu_parts(values):
    sig = jax.nn.sigmoid(values)
    return (values * sig, sig * (1.0 + values * (1.0 - sig)))

def span_pass(queries, keys_here, values_here, rates, gate_low, up_low, down_low, heads):
    count = queries.shape[0]
    width = gate_low.shape[1]
    hidden = gate_low.shape[0] // heads
    gate_three = gate_low.astype(jnp.float32).reshape(heads, hidden, width)
    up_three = up_low.astype(jnp.float32).reshape(heads, hidden, width)
    down_three = down_low.astype(jnp.float32).reshape(heads, width, hidden)
    key_three = keys_here.astype(jnp.float32).reshape(count, heads, width)
    first = jnp.einsum('thd,hfd->thf', key_three, gate_three)
    second = jnp.einsum('thd,hfd->thf', key_three, up_three)
    silu_first, slope = silu_parts(first)
    acts = (silu_first * second).astype(jnp.bfloat16)
    scaled = (rates[:, :, None] * values_here.astype(jnp.float32).reshape(count, heads, width)).astype(jnp.bfloat16)
    back = jnp.einsum('thd,hdf->thf', scaled.astype(jnp.float32), down_three)
    d_gate = (back * second * slope).astype(jnp.bfloat16)
    d_up = (back * silu_first).astype(jnp.bfloat16)
    grad_gate = jnp.einsum('thf,thd->hfd', d_gate.astype(jnp.float32), key_three).reshape(heads * hidden, width)
    grad_up = jnp.einsum('thf,thd->hfd', d_up.astype(jnp.float32), key_three).reshape(heads * hidden, width)
    grad_down = jnp.einsum('thd,thf->hdf', scaled.astype(jnp.float32), acts.astype(jnp.float32)).reshape(heads * width, hidden)
    query_three = queries.astype(jnp.float32).reshape(count, heads, width)
    query_gate = jnp.einsum('thd,hfd->thf', query_three, gate_three)
    query_up = jnp.einsum('thd,hfd->thf', query_three, up_three)
    query_acts = (jax.nn.silu(query_gate) * query_up).astype(jnp.bfloat16)
    output = jnp.einsum('thf,hdf->thd', query_acts.astype(jnp.float32), down_three)
    return (output.reshape(count, heads * width).astype(jnp.bfloat16), (grad_gate, grad_up, grad_down))

def refresh(matrix, gradient, heads):
    total_rows, columns = matrix.shape
    grad_three = gradient.reshape(heads, total_rows // heads, columns)
    block_mean = lax.optimization_barrier(jnp.mean(grad_three * grad_three, axis=(1, 2)))
    factor = lax.rsqrt(block_mean + 1e-06) / math.sqrt(columns)
    stepped = matrix + (grad_three * factor[:, None, None]).reshape(total_rows, columns)
    row_mean = lax.optimization_barrier(jnp.mean(stepped * stepped, axis=1, keepdims=True))
    return stepped * lax.rsqrt(row_mean + 1e-06) / math.sqrt(columns)

def reference(query_rows, key_rows, value_rows, step_rates, gate_weight, up_weight, down_weight):
    heads = step_rates.shape[2]
    masters = (gate_weight, up_weight, down_weight)
    results = []
    for span_index in range(SPANS):
        lowered = tuple((matrix.astype(jnp.bfloat16) for matrix in masters))
        output, grads = span_pass(query_rows[span_index], key_rows[span_index], value_rows[span_index], step_rates[span_index], lowered[0], lowered[1], lowered[2], heads)
        results.append(output)
        masters = tuple((refresh(masters[i], grads[i], heads) for i in range(3)))
    return (jnp.stack(results), masters[0], masters[1], masters[2])
```

```python
import functools
import math

import jax
import jax.numpy as jnp
from jax import lax
from jax.experimental import pallas as pl
from jax.experimental.pallas import tpu as pltpu
from jax.sharding import PartitionSpec as P


def from_partner(value, axis, apart):
    mask = 2**apart
    pairs = [(source, source ^ mask) for source in range(lax.axis_size(axis))]
    return lax.ppermute(value, axis, pairs)


def silu_parts(values):
    sig = jax.nn.sigmoid(values)
    return (values * sig, sig * (1.0 + values * (1.0 - sig)))


def span_pass(queries, keys_here, scaled_rows, gate_low, up_low, down_low, heads):
    count = queries.shape[0]
    width = gate_low.shape[1]
    hidden = gate_low.shape[0] // heads
    gate_three = gate_low.reshape(heads, hidden, width)
    up_three = up_low.reshape(heads, hidden, width)
    down_three = down_low.reshape(heads, width, hidden)
    key_three = keys_here.reshape(count, heads, width)
    first = jnp.einsum("thd,hfd->thf", key_three, gate_three, preferred_element_type=jnp.float32)
    second = jnp.einsum("thd,hfd->thf", key_three, up_three, preferred_element_type=jnp.float32)
    silu_first, slope = silu_parts(first)
    acts = (silu_first * second).astype(jnp.bfloat16)
    scaled = scaled_rows.reshape(count, heads, width)
    back = jnp.einsum("thd,hdf->thf", scaled, down_three, preferred_element_type=jnp.float32)
    d_gate = (back * second * slope).astype(jnp.bfloat16)
    d_up = (back * silu_first).astype(jnp.bfloat16)
    grad_gate = jnp.einsum(
        "thf,thd->hfd", d_gate, key_three, preferred_element_type=jnp.float32
    ).reshape(heads * hidden, width)
    grad_up = jnp.einsum(
        "thf,thd->hfd", d_up, key_three, preferred_element_type=jnp.float32
    ).reshape(heads * hidden, width)
    grad_down = jnp.einsum(
        "thd,thf->hdf", scaled, acts, preferred_element_type=jnp.float32
    ).reshape(heads * width, hidden)
    query_three = queries.reshape(count, heads, width)
    query_gate = jnp.einsum(
        "thd,hfd->thf", query_three, gate_three, preferred_element_type=jnp.float32
    )
    query_up = jnp.einsum("thd,hfd->thf", query_three, up_three, preferred_element_type=jnp.float32)
    query_acts = (jax.nn.silu(query_gate) * query_up).astype(jnp.bfloat16)
    output = jnp.einsum("thf,hdf->thd", query_acts, down_three, preferred_element_type=jnp.float32)
    return (
        output.reshape(count, heads * width).astype(jnp.bfloat16),
        (grad_gate, grad_up, grad_down),
    )


def head_member(row_count, offset, per_head, heads):
    row_ids = offset + jnp.arange(row_count, dtype=jnp.int32)
    head_ids = jnp.arange(heads, dtype=jnp.int32)
    return (row_ids[:, None] // per_head == head_ids[None, :]).astype(jnp.float32)


def head_partial(gradient, member):
    return jnp.sum(member * jnp.sum(gradient * gradient, axis=1)[:, None], axis=0)


def refresh_rows(matrix, gradient, member, head_total, per_head):
    columns = matrix.shape[1]
    block_mean = head_total / (per_head * columns)
    factor = lax.rsqrt(block_mean + 1e-06) / math.sqrt(columns)
    row_factor = jnp.sum(member * factor[None, :], axis=1)
    stepped = matrix + gradient * row_factor[:, None]
    row_mean = jnp.mean(stepped * stepped, axis=1, keepdims=True)
    return stepped * lax.rsqrt(row_mean + 1e-06) / math.sqrt(columns)


def update_shards(masters, shares, heads):
    row_count = masters[0].shape[0]
    total_rows = row_count * lax.axis_size("ctx")
    per_head = total_rows // heads
    offset = lax.axis_index("ctx") * row_count
    member = head_member(row_count, offset, per_head, heads)
    partials = [head_partial(shares[i], member) for i in range(3)]
    totals = lax.psum((partials[0], partials[1], partials[2]), "ctx")
    return tuple(
        (refresh_rows(masters[i], shares[i], member, totals[i], per_head) for i in range(3))
    )


def scale_values(value_rows, step_rates):
    span_count, count, total_width = value_rows.shape
    heads = step_rates.shape[2]
    spread = value_rows.reshape(span_count, count, heads, total_width // heads).astype(jnp.float32)
    return (
        (step_rates[:, :, :, None] * spread)
        .astype(jnp.bfloat16)
        .reshape(span_count, count, total_width)
    )


def to_heads(array, groups, heads):
    span_count, count, total_width = array.shape
    slab = count // groups
    width = total_width // heads
    spread = array.reshape(span_count, groups, slab, heads, width).transpose(3, 1, 0, 2, 4)
    return spread.reshape(heads * groups, span_count, slab, width)


def from_heads(array, groups, heads):
    devices, span_count, slab, width = array.shape
    spread = array.reshape(heads, groups, span_count, slab, width).transpose(2, 1, 3, 0, 4)
    return spread.reshape(span_count, groups * slab, heads * width)


def per_device_general(query_rows, key_rows, value_rows, step_rates, gate_weight, up_weight, down_weight):
    heads = step_rates.shape[2]
    span_count = query_rows.shape[0]
    scaled_all = scale_values(value_rows, step_rates)
    results = []
    groups = lax.axis_size("ctx") // heads
    bits = groups.bit_length() - 1
    position = lax.axis_index("ctx")
    moved = (
        lax.all_to_all(
            to_heads(query_rows, groups, heads), "ctx", split_axis=0, concat_axis=0, tiled=True
        ),
        lax.all_to_all(
            to_heads(key_rows, groups, heads), "ctx", split_axis=0, concat_axis=0, tiled=True
        ),
        lax.all_to_all(
            to_heads(scaled_all, groups, heads), "ctx", split_axis=0, concat_axis=0, tiled=True
        ),
    )
    width = moved[0].shape[3]
    masters = (gate_weight, up_weight, down_weight)
    for span_index in range(span_count):
        blocks = tuple((matrix.astype(jnp.bfloat16) for matrix in masters))
        for level in range(bits):
            other = from_partner((blocks[0], blocks[1], blocks[2]), "ctx", level)
            upper_side = position >> level & 1 == 1
            blocks = tuple(
                (
                    jnp.where(
                        upper_side,
                        jnp.concatenate([other[i], blocks[i]], axis=0),
                        jnp.concatenate([blocks[i], other[i]], axis=0),
                    )
                    for i in range(3)
                )
            )
        queries = moved[0][:, span_index].reshape(-1, width)
        keys_here = moved[1][:, span_index].reshape(-1, width)
        scaled_rows = moved[2][:, span_index].reshape(-1, width)
        output, grads = span_pass(
            queries, keys_here, scaled_rows, blocks[0], blocks[1], blocks[2], 1
        )
        results.append(output.reshape(moved[0].shape[0], moved[0].shape[2], width))
        for level in reversed(range(bits)):
            upper_side = position >> level & 1 == 1
            halves = [grad.shape[0] // 2 for grad in grads]
            kept = tuple(
                (
                    jnp.where(upper_side, grads[i][halves[i] :], grads[i][: halves[i]])
                    for i in range(3)
                )
            )
            sent = tuple(
                (
                    jnp.where(upper_side, grads[i][: halves[i]], grads[i][halves[i] :])
                    for i in range(3)
                )
            )
            other = from_partner((sent[0], sent[1], sent[2]), "ctx", level)
            grads = tuple((kept[i] + other[i] for i in range(3)))
        masters = update_shards(masters, grads, heads)
    stacked = jnp.stack(results, axis=1)
    returned = lax.all_to_all(stacked, "ctx", split_axis=0, concat_axis=0, tiled=True)
    return (from_heads(returned, groups, heads), masters[0], masters[1], masters[2])


def mm(left, right, left_dim, right_dim):
    return lax.dot_general(
        left,
        right,
        (((left_dim,), (right_dim,)), ((), ())),
        preferred_element_type=jnp.float32,
    )


def sigmoid(values):
    return 0.5 * jnp.tanh(0.5 * values) + 0.5


def fused_kernel(
    heads,
    groups,
    q_ref,
    k_ref,
    v_ref,
    r_ref,
    gate_ref,
    up_ref,
    down_ref,
    att_ref,
    gate_out,
    up_out,
    down_out,
    scaled_buf,
    tok,
    out_buf,
    low,
    low_grad,
    grad,
    grad_in,
    master,
    total,
    d_gate,
    d_up,
    acts,
    square,
    square_in,
    tok_send,
    tok_recv,
    att_send,
    att_recv,
    low_send,
    low_recv,
    grad_send,
    grad_recv,
    square_send,
    square_recv,
):
    spans, count, _ = q_ref.shape
    rows, width = gate_ref.shape
    position = lax.axis_index("ctx")
    head = lax.div(position, groups)
    member = lax.rem(position, groups)

    def across(step):
        return lax.rem(head + step, heads)

    def within(step):
        return lax.rem(member + step, groups)

    def far(which):
        return {"ctx": which * groups + member}

    def near(which):
        return {"ctx": head * groups + which}

    def columns(which):
        return pl.ds(pl.multiple_of(which * width, 128), width)

    def rows_of(which):
        return pl.ds(pl.multiple_of(which * rows, 16), rows)

    own_rows = rows_of(member)
    own_columns = columns(head)

    barrier = pltpu.get_barrier_semaphore()
    for step in range(1, heads):
        pl.semaphore_signal(
            barrier, inc=1, device_id=far(across(step)), device_id_type=pl.DeviceIdType.MESH
        )
    for step in range(1, groups):
        pl.semaphore_signal(
            barrier, inc=1, device_id=near(within(step)), device_id_type=pl.DeviceIdType.MESH
        )

    def scale(span):
        for each in range(heads):
            part = v_ref[span, :, each * width : (each + 1) * width].astype(jnp.float32)
            rate = r_ref[span, :, each : each + 1]
            scaled_buf[span, :, each * width : (each + 1) * width] = (part * rate).astype(
                jnp.bfloat16
            )

    def token_copy(span, kind, source_at, slot, target):
        source = (q_ref, k_ref, scaled_buf)[kind]
        return pltpu.make_async_remote_copy(
            src_ref=source.at[span, :, columns(source_at)],
            dst_ref=tok.at[span, kind, slot],
            send_sem=tok_send.at[span, kind, target],
            recv_sem=tok_recv.at[span, kind, slot],
            device_id=far(target),
            device_id_type=pl.DeviceIdType.MESH,
        )

    def send_tokens(span, kind):
        for step in range(1, heads):
            target = across(step)
            token_copy(span, kind, target, head, target).start()

    def wait_tokens(span, kind, source):
        token_copy(span, kind, source, source, source).wait_recv()

    def own_tokens(span, kind):
        source = (q_ref, k_ref, scaled_buf)[kind]
        tok[span, kind, head] = source[span, :, own_columns]

    def att_copy(span, slot, column, target):
        return pltpu.make_async_remote_copy(
            src_ref=out_buf.at[span, slot],
            dst_ref=att_ref.at[span, :, columns(column)],
            send_sem=att_send.at[span, slot],
            recv_sem=att_recv.at[span, column],
            device_id=far(target),
            device_id_type=pl.DeviceIdType.MESH,
        )

    def low_copy(span, which, block, target):
        return pltpu.make_async_remote_copy(
            src_ref=low.at[span, which, rows_of(block)],
            dst_ref=low.at[span, which, rows_of(block)],
            send_sem=low_send.at[span, which, target],
            recv_sem=low_recv.at[span, which, block],
            device_id=near(target),
            device_id_type=pl.DeviceIdType.MESH,
        )

    def grad_copy(span, which, slot, target):
        return pltpu.make_async_remote_copy(
            src_ref=low_grad.at[span, which, rows_of(target)],
            dst_ref=grad_in.at[span, which, slot],
            send_sem=grad_send.at[span, which, target],
            recv_sem=grad_recv.at[span, which, slot],
            device_id=near(target),
            device_id_type=pl.DeviceIdType.MESH,
        )

    def square_copy(span, slot, target):
        return pltpu.make_async_remote_copy(
            src_ref=square.at[span],
            dst_ref=square_in.at[span, slot],
            send_sem=square_send.at[span, target],
            recv_sem=square_recv.at[span, slot],
            device_id=near(target),
            device_id_type=pl.DeviceIdType.MESH,
        )

    def send_low(span, which):
        for step in range(1, groups):
            target = within(step)
            low_copy(span, which, member, target).start()

    weights = (gate_ref, up_ref, down_ref)
    finals = (gate_out, up_out, down_out)
    for which in range(3):
        low[0, which, own_rows] = weights[which][...].astype(jnp.bfloat16)
    scale(0)
    pl.semaphore_wait(barrier, heads + groups - 2)
    send_tokens(0, 1)
    send_tokens(0, 2)
    for which in range(3):
        send_low(0, which)
    for span in range(1, spans):
        scale(span)
    for span in range(spans):
        for kind in range(3):
            own_tokens(span, kind)
    for span in range(spans):
        for kind in ((0,) if span == 0 else (1, 2, 0)):
            send_tokens(span, kind)

    for span in range(spans):
        for step in range(1, groups):
            source = within(step)
            for which in range(3):
                low_copy(span, which, source, source).wait_recv()

        def forward(step, carry):
            slot = lax.rem(head + step, heads)

            @pl.when(step > 0)
            def _():
                wait_tokens(span, 1, slot)
                wait_tokens(span, 2, slot)

            keys = tok[span, 1, slot]
            first = mm(keys, low[span, 0], 1, 1)
            second = mm(keys, low[span, 1], 1, 1)
            back = mm(tok[span, 2, slot], low[span, 2], 1, 0)
            sig = sigmoid(first)
            silu_first = first * sig
            slope = sig * (1.0 + first * (1.0 - sig))
            acts[slot] = (silu_first * second).astype(jnp.bfloat16)
            d_gate[slot] = (back * second * slope).astype(jnp.bfloat16)
            d_up[slot] = (back * silu_first).astype(jnp.bfloat16)
            return carry

        lax.fori_loop(0, heads, forward, 0)
        keys = tok[span, 1].reshape(heads * count, width)
        scaled = tok[span, 2].reshape(heads * count, width)
        pairs = (
            (d_gate[...].reshape(heads * count, -1), keys),
            (d_up[...].reshape(heads * count, -1), keys),
            (scaled, acts[...].reshape(heads * count, -1)),
        )
        for which in range(3):
            product = mm(pairs[which][0], pairs[which][1], 0, 0)
            grad[which] = product
            low_grad[span, which] = product.astype(jnp.bfloat16)
            for step in range(1, groups):
                target = within(step)
                grad_copy(span, which, member, target).start()

        def answer(step, carry):
            slot = lax.rem(head + step, heads)

            @pl.when(step > 0)
            def _():
                wait_tokens(span, 0, slot)

            queries = tok[span, 0, slot]
            first = mm(queries, low[span, 0], 1, 1)
            second = mm(queries, low[span, 1], 1, 1)
            hidden = (first * sigmoid(first) * second).astype(jnp.bfloat16)
            out_buf[span, slot] = mm(hidden, low[span, 2], 1, 1).astype(jnp.bfloat16)

            @pl.when(step > 0)
            def _():
                att_copy(span, slot, head, slot).start()

            return carry

        def collect():
            for which in range(3):
                summed = grad[which, own_rows]
                for step in range(1, groups):
                    source = within(step)
                    grad_copy(span, which, source, source).wait_recv()
                    summed = summed + grad_in[span, which, source].astype(jnp.float32)
                total[which] = summed
                squared = summed * summed
                by_row = jnp.sum(squared.reshape(rows // 8, 8, width), axis=0)
                lanes = by_row[:, :128]
                for at in range(128, width, 128):
                    lanes = lanes + by_row[:, at : at + 128]
                square[span, which] = lanes
            for step in range(1, groups):
                square_copy(span, member, within(step)).start()

        def refresh():
            for step in range(1, groups):
                source = within(step)
                square_copy(span, source, source).wait_recv()
            for which in range(3):
                sums = square[span, which]
                for step in range(1, groups):
                    sums = sums + square_in[span, within(step), which]
                block_mean = jnp.sum(sums, keepdims=True) / (rows * groups * width)
                factor = lax.rsqrt(block_mean + 1e-06) / math.sqrt(width)
                before = weights[which][...] if span == 0 else master[which]
                stepped = before + total[which] * factor
                row_mean = jnp.mean(stepped * stepped, axis=1, keepdims=True)
                after = stepped * (lax.rsqrt(row_mean + 1e-06) / math.sqrt(width))
                if span == spans - 1:
                    finals[which][...] = after
                else:
                    master[which] = after
                    low[span + 1, which, own_rows] = after.astype(jnp.bfloat16)
                    send_low(span + 1, which)

        lax.fori_loop(0, heads, answer, 0)
        collect()
        refresh()
        att_ref[span, :, own_columns] = out_buf[span, head]

    for span in range(spans):
        for step in range(1, heads):
            other = across(step)
            att_copy(span, other, other, other).wait_recv()
            att_copy(span, other, other, other).wait_send()
            for kind in range(3):
                token_copy(span, kind, other, other, other).wait_send()
        for step in range(1, groups):
            other = within(step)
            for which in range(3):
                low_copy(span, which, other, other).wait_send()
                grad_copy(span, which, other, other).wait_send()
            square_copy(span, other, other).wait_send()


def per_device_fused(
    heads, groups, query_rows, key_rows, value_rows, step_rates, gate_weight, up_weight, down_weight
):
    spans, count, full = query_rows.shape
    rows, width = gate_weight.shape
    block = rows * groups
    low = jnp.bfloat16
    vmem = pl.BlockSpec(memory_space=pltpu.VMEM)
    weight = jax.ShapeDtypeStruct((rows, width), jnp.float32)
    dma = pltpu.SemaphoreType.DMA
    return pl.pallas_call(
        functools.partial(fused_kernel, heads, groups),
        out_shape=(
            jax.ShapeDtypeStruct((spans, count, full), low),
            weight,
            weight,
            weight,
        ),
        in_specs=[vmem] * 7,
        out_specs=(vmem,) * 4,
        scratch_shapes=[
            pltpu.VMEM((spans, count, full), low),
            pltpu.VMEM((spans, 3, heads, count, width), low),
            pltpu.VMEM((spans, heads, count, width), low),
            pltpu.VMEM((spans, 3, block, width), low),
            pltpu.VMEM((spans, 3, block, width), low),
            pltpu.VMEM((3, block, width), jnp.float32),
            pltpu.VMEM((spans, 3, groups, rows, width), low),
            pltpu.VMEM((3, rows, width), jnp.float32),
            pltpu.VMEM((3, rows, width), jnp.float32),
            pltpu.VMEM((heads, count, width), low),
            pltpu.VMEM((heads, count, width), low),
            pltpu.VMEM((heads, count, width), low),
            pltpu.VMEM((spans, 3, 8, 128), jnp.float32),
            pltpu.VMEM((spans, groups, 3, 8, 128), jnp.float32),
            dma((spans, 3, heads)),
            dma((spans, 3, heads)),
            dma((spans, heads)),
            dma((spans, heads)),
            dma((spans, 3, groups)),
            dma((spans, 3, groups)),
            dma((spans, 3, groups)),
            dma((spans, 3, groups)),
            dma((spans, groups)),
            dma((spans, groups)),
        ],
        compiler_params=pltpu.CompilerParams(
            collective_id=0, has_side_effects=True, vmem_limit_bytes=40 * 2**20
        ),
    )(query_rows, key_rows, value_rows, step_rates, gate_weight, up_weight, down_weight)


def per_device(query_rows, key_rows, value_rows, step_rates, gate_weight, up_weight, down_weight):
    arguments = (
        query_rows, key_rows, value_rows, step_rates, gate_weight, up_weight, down_weight
    )
    heads = step_rates.shape[2]
    size = lax.axis_size("ctx")
    rows, width = gate_weight.shape
    count = query_rows.shape[1]
    groups = size // heads
    fits = (
        size % heads == 0
        and down_weight.shape == gate_weight.shape
        and rows * groups == width
        and query_rows.shape[2] == heads * width
        and rows % 16 == 0
        and width % 128 == 0
        and count % 16 == 0
        and 2 <= groups <= 8
    )
    if fits:
        return per_device_fused(heads, groups, *arguments)
    return per_device_general(*arguments)


def solution(mesh):
    placed = (
        P(None, ("parts", "ctx"), None),
        P(None, ("parts", "ctx"), None),
        P(None, ("parts", "ctx"), None),
        P(None, ("parts", "ctx"), None),
        P(("parts", "ctx"), None),
        P(("parts", "ctx"), None),
        P(("parts", "ctx"), None),
    )
    return jax.shard_map(
        per_device,
        mesh=mesh,
        in_specs=placed,
        out_specs=(
            P(None, ("parts", "ctx"), None),
            P(("parts", "ctx"), None),
            P(("parts", "ctx"), None),
            P(("parts", "ctx"), None),
        ),
        check_vma=False,
    )
```

```python
import functools
import math

import jax
import jax.numpy as jnp
from jax import lax
from jax.experimental import pallas as pl
from jax.experimental.pallas import tpu as pltpu
from jax.sharding import PartitionSpec as P


def from_partner(value, axis, apart):
    mask = 2**apart
    pairs = [(source, source ^ mask) for source in range(lax.axis_size(axis))]
    return lax.ppermute(value, axis, pairs)


def silu_parts(values):
    sig = jax.nn.sigmoid(values)
    return (values * sig, sig * (1.0 + values * (1.0 - sig)))


def span_pass(queries, keys_here, scaled_rows, gate_low, up_low, down_low, heads):
    count = queries.shape[0]
    width = gate_low.shape[1]
    hidden = gate_low.shape[0] // heads
    gate_three = gate_low.reshape(heads, hidden, width)
    up_three = up_low.reshape(heads, hidden, width)
    down_three = down_low.reshape(heads, width, hidden)
    key_three = keys_here.reshape(count, heads, width)
    first = jnp.einsum("thd,hfd->thf", key_three, gate_three, preferred_element_type=jnp.float32)
    second = jnp.einsum("thd,hfd->thf", key_three, up_three, preferred_element_type=jnp.float32)
    silu_first, slope = silu_parts(first)
    acts = (silu_first * second).astype(jnp.bfloat16)
    scaled = scaled_rows.reshape(count, heads, width)
    back = jnp.einsum("thd,hdf->thf", scaled, down_three, preferred_element_type=jnp.float32)
    d_gate = (back * second * slope).astype(jnp.bfloat16)
    d_up = (back * silu_first).astype(jnp.bfloat16)
    grad_gate = jnp.einsum(
        "thf,thd->hfd", d_gate, key_three, preferred_element_type=jnp.float32
    ).reshape(heads * hidden, width)
    grad_up = jnp.einsum(
        "thf,thd->hfd", d_up, key_three, preferred_element_type=jnp.float32
    ).reshape(heads * hidden, width)
    grad_down = jnp.einsum(
        "thd,thf->hdf", scaled, acts, preferred_element_type=jnp.float32
    ).reshape(heads * width, hidden)
    query_three = queries.reshape(count, heads, width)
    query_gate = jnp.einsum(
        "thd,hfd->thf", query_three, gate_three, preferred_element_type=jnp.float32
    )
    query_up = jnp.einsum("thd,hfd->thf", query_three, up_three, preferred_element_type=jnp.float32)
    query_acts = (jax.nn.silu(query_gate) * query_up).astype(jnp.bfloat16)
    output = jnp.einsum("thf,hdf->thd", query_acts, down_three, preferred_element_type=jnp.float32)
    return (
        output.reshape(count, heads * width).astype(jnp.bfloat16),
        (grad_gate, grad_up, grad_down),
    )


def head_member(row_count, offset, per_head, heads):
    row_ids = offset + jnp.arange(row_count, dtype=jnp.int32)
    head_ids = jnp.arange(heads, dtype=jnp.int32)
    return (row_ids[:, None] // per_head == head_ids[None, :]).astype(jnp.float32)


def head_partial(gradient, member):
    return jnp.sum(member * jnp.sum(gradient * gradient, axis=1)[:, None], axis=0)


def refresh_rows(matrix, gradient, member, head_total, per_head):
    columns = matrix.shape[1]
    block_mean = head_total / (per_head * columns)
    factor = lax.rsqrt(block_mean + 1e-06) / math.sqrt(columns)
    row_factor = jnp.sum(member * factor[None, :], axis=1)
    stepped = matrix + gradient * row_factor[:, None]
    row_mean = jnp.mean(stepped * stepped, axis=1, keepdims=True)
    return stepped * lax.rsqrt(row_mean + 1e-06) / math.sqrt(columns)


def update_shards(masters, shares, heads):
    row_count = masters[0].shape[0]
    total_rows = row_count * lax.axis_size("ctx")
    per_head = total_rows // heads
    offset = lax.axis_index("ctx") * row_count
    member = head_member(row_count, offset, per_head, heads)
    partials = [head_partial(shares[i], member) for i in range(3)]
    totals = lax.psum((partials[0], partials[1], partials[2]), "ctx")
    return tuple(
        (refresh_rows(masters[i], shares[i], member, totals[i], per_head) for i in range(3))
    )


def scale_values(value_rows, step_rates):
    span_count, count, total_width = value_rows.shape
    heads = step_rates.shape[2]
    spread = value_rows.reshape(span_count, count, heads, total_width // heads).astype(jnp.float32)
    return (
        (step_rates[:, :, :, None] * spread)
        .astype(jnp.bfloat16)
        .reshape(span_count, count, total_width)
    )


def to_heads(array, groups, heads):
    span_count, count, total_width = array.shape
    slab = count // groups
    width = total_width // heads
    spread = array.reshape(span_count, groups, slab, heads, width).transpose(3, 1, 0, 2, 4)
    return spread.reshape(heads * groups, span_count, slab, width)


def from_heads(array, groups, heads):
    devices, span_count, slab, width = array.shape
    spread = array.reshape(heads, groups, span_count, slab, width).transpose(2, 1, 3, 0, 4)
    return spread.reshape(span_count, groups * slab, heads * width)


def per_device_general(query_rows, key_rows, value_rows, step_rates, gate_weight, up_weight, down_weight):
    heads = step_rates.shape[2]
    span_count = query_rows.shape[0]
    scaled_all = scale_values(value_rows, step_rates)
    results = []
    groups = lax.axis_size("ctx") // heads
    bits = groups.bit_length() - 1
    position = lax.axis_index("ctx")
    moved = (
        lax.all_to_all(
            to_heads(query_rows, groups, heads), "ctx", split_axis=0, concat_axis=0, tiled=True
        ),
        lax.all_to_all(
            to_heads(key_rows, groups, heads), "ctx", split_axis=0, concat_axis=0, tiled=True
        ),
        lax.all_to_all(
            to_heads(scaled_all, groups, heads), "ctx", split_axis=0, concat_axis=0, tiled=True
        ),
    )
    width = moved[0].shape[3]
    masters = (gate_weight, up_weight, down_weight)
    for span_index in range(span_count):
        blocks = tuple((matrix.astype(jnp.bfloat16) for matrix in masters))
        for level in range(bits):
            other = from_partner((blocks[0], blocks[1], blocks[2]), "ctx", level)
            upper_side = position >> level & 1 == 1
            blocks = tuple(
                (
                    jnp.where(
                        upper_side,
                        jnp.concatenate([other[i], blocks[i]], axis=0),
                        jnp.concatenate([blocks[i], other[i]], axis=0),
                    )
                    for i in range(3)
                )
            )
        queries = moved[0][:, span_index].reshape(-1, width)
        keys_here = moved[1][:, span_index].reshape(-1, width)
        scaled_rows = moved[2][:, span_index].reshape(-1, width)
        output, grads = span_pass(
            queries, keys_here, scaled_rows, blocks[0], blocks[1], blocks[2], 1
        )
        results.append(output.reshape(moved[0].shape[0], moved[0].shape[2], width))
        for level in reversed(range(bits)):
            upper_side = position >> level & 1 == 1
            halves = [grad.shape[0] // 2 for grad in grads]
            kept = tuple(
                (
                    jnp.where(upper_side, grads[i][halves[i] :], grads[i][: halves[i]])
                    for i in range(3)
                )
            )
            sent = tuple(
                (
                    jnp.where(upper_side, grads[i][: halves[i]], grads[i][halves[i] :])
                    for i in range(3)
                )
            )
            other = from_partner((sent[0], sent[1], sent[2]), "ctx", level)
            grads = tuple((kept[i] + other[i] for i in range(3)))
        masters = update_shards(masters, grads, heads)
    stacked = jnp.stack(results, axis=1)
    returned = lax.all_to_all(stacked, "ctx", split_axis=0, concat_axis=0, tiled=True)
    return (from_heads(returned, groups, heads), masters[0], masters[1], masters[2])


PIECES = 2


def mm(left, right, left_dim, right_dim):
    return lax.dot_general(
        left,
        right,
        (((left_dim,), (right_dim,)), ((), ())),
        preferred_element_type=jnp.float32,
    )


def sigmoid(values):
    return 0.5 * jnp.tanh(0.5 * values) + 0.5


def fused_kernel(
    heads,
    groups,
    q_ref,
    k_ref,
    v_ref,
    r_ref,
    gate_ref,
    up_ref,
    down_ref,
    att_ref,
    gate_out,
    up_out,
    down_out,
    scaled_buf,
    tok,
    tok_query,
    out_buf,
    low,
    low_grad,
    grad,
    grad_in,
    master,
    total,
    d_gate,
    d_up,
    acts,
    square,
    square_in,
    tok_send,
    tok_recv,
    query_send,
    query_recv,
    att_send,
    att_recv,
    chain_send,
    chain_recv,
    low_send,
    low_recv,
    grad_send,
    grad_recv,
    square_send,
    square_recv,
):
    spans, count, _ = q_ref.shape
    rows, width = gate_ref.shape
    position = lax.axis_index("ctx")
    head = lax.div(position, groups)
    member = lax.rem(position, groups)

    half = heads // 2
    piece = low.shape[3] // PIECES

    def query_head(which):
        return lax.rem(which, 2) * half + lax.div(which, 2)

    quest = query_head(member)
    apart = (head - quest) * (head - quest)
    held = lax.div(apart + heads * heads - 1, heads * heads)

    def across(step):
        return lax.rem(head + step, heads)

    def within(step):
        return lax.rem(member + step, groups)

    def far(which):
        return {"ctx": which * groups + member}

    def near(which):
        return {"ctx": head * groups + which}

    def columns(which):
        return pl.ds(pl.multiple_of(which * width, 128), width)

    def rows_of(which):
        return pl.ds(pl.multiple_of(which * rows, 16), rows)

    own_rows = rows_of(member)
    own_columns = columns(head)

    barrier = pltpu.get_barrier_semaphore()
    for step in range(1, heads):
        pl.semaphore_signal(
            barrier, inc=1, device_id=far(across(step)), device_id_type=pl.DeviceIdType.MESH
        )
    for step in range(1, groups):
        pl.semaphore_signal(
            barrier, inc=1, device_id=near(within(step)), device_id_type=pl.DeviceIdType.MESH
        )

    def scale(span):
        for each in range(heads):
            part = v_ref[span, :, each * width : (each + 1) * width].astype(jnp.float32)
            rate = r_ref[span, :, each : each + 1]
            scaled_buf[span, :, each * width : (each + 1) * width] = (part * rate).astype(
                jnp.bfloat16
            )

    def token_copy(span, kind, source_at, slot, target):
        source = (k_ref, scaled_buf)[kind]
        return pltpu.make_async_remote_copy(
            src_ref=source.at[span, :, columns(source_at)],
            dst_ref=tok.at[span, kind, slot],
            send_sem=tok_send.at[span, kind, target],
            recv_sem=tok_recv.at[span, kind, slot],
            device_id=far(target),
            device_id_type=pl.DeviceIdType.MESH,
        )

    def send_tokens(span, kind):
        for step in range(1, heads):
            target = across(step)
            token_copy(span, kind, target, head, target).start()

    def wait_tokens(span, kind, source):
        token_copy(span, kind, source, source, source).wait_recv()

    def own_tokens(span, kind):
        source = (k_ref, scaled_buf)[kind]
        tok[span, kind, head] = source[span, :, own_columns]

    def query_copy(span, column, slot, target):
        return pltpu.make_async_remote_copy(
            src_ref=q_ref.at[span, :, columns(column)],
            dst_ref=tok_query.at[span, slot],
            send_sem=query_send.at[span, target],
            recv_sem=query_recv.at[span, slot],
            device_id=near(target),
            device_id_type=pl.DeviceIdType.MESH,
        )

    def send_queries(span):
        for step in range(1, groups):
            target = within(step)
            query_copy(span, query_head(target), member, target).start()

    def att_copy(span, slot, column, source, target):
        return pltpu.make_async_remote_copy(
            src_ref=out_buf.at[span, slot],
            dst_ref=att_ref.at[span, :, columns(column)],
            send_sem=att_send.at[span, slot],
            recv_sem=att_recv.at[span, source],
            device_id=near(target),
            device_id_type=pl.DeviceIdType.MESH,
        )

    def send_att(span):
        for step in range(1, groups):
            target = within(step)
            att_copy(span, target, quest, member, target).start()

    def chain_copy(span, which, part, side, target):
        cut = pl.ds(part * piece, piece)
        return pltpu.make_async_remote_copy(
            src_ref=low.at[span, held, which, cut],
            dst_ref=low.at[span, 1, which, cut],
            send_sem=chain_send.at[span, which, part, side],
            recv_sem=chain_recv.at[span, which, part],
            device_id=far(target),
            device_id_type=pl.DeviceIdType.MESH,
        )

    def chain_start(span, which):
        @pl.when(head == quest)
        def _():
            for part in range(PIECES):

                @pl.when(head < heads - 1)
                def _():
                    chain_copy(span, which, part, 0, head + 1).start()

                @pl.when(head > 0)
                def _():
                    chain_copy(span, which, part, 1, head - 1).start()

    def chain_pass(span, which):
        for part in range(PIECES):

            @pl.when(head > quest)
            def _():
                chain_copy(span, which, part, 0, head - 1).wait_recv()

                @pl.when(head < heads - 1)
                def _():
                    chain_copy(span, which, part, 0, head + 1).start()

            @pl.when(head < quest)
            def _():
                chain_copy(span, which, part, 1, head + 1).wait_recv()

                @pl.when(head > 0)
                def _():
                    chain_copy(span, which, part, 1, head - 1).start()

    def chain_finish(span, which):
        for part in range(PIECES):

            @pl.when((head >= quest) & (head < heads - 1))
            def _():
                chain_copy(span, which, part, 0, head + 1).wait_send()

            @pl.when((head <= quest) & (head > 0))
            def _():
                chain_copy(span, which, part, 1, head - 1).wait_send()

    def low_copy(span, which, block, target):
        return pltpu.make_async_remote_copy(
            src_ref=low.at[span, 0, which, rows_of(block)],
            dst_ref=low.at[span, 0, which, rows_of(block)],
            send_sem=low_send.at[span, which, target],
            recv_sem=low_recv.at[span, which, block],
            device_id=near(target),
            device_id_type=pl.DeviceIdType.MESH,
        )

    def grad_copy(span, which, slot, target):
        return pltpu.make_async_remote_copy(
            src_ref=low_grad.at[span, which, rows_of(target)],
            dst_ref=grad_in.at[span, which, slot],
            send_sem=grad_send.at[span, which, target],
            recv_sem=grad_recv.at[span, which, slot],
            device_id=near(target),
            device_id_type=pl.DeviceIdType.MESH,
        )

    def square_copy(span, slot, target):
        return pltpu.make_async_remote_copy(
            src_ref=square.at[span],
            dst_ref=square_in.at[span, slot],
            send_sem=square_send.at[span, target],
            recv_sem=square_recv.at[span, slot],
            device_id=near(target),
            device_id_type=pl.DeviceIdType.MESH,
        )

    def send_low(span, which):
        for step in range(1, groups):
            target = within(step)
            low_copy(span, which, member, target).start()

    weights = (gate_ref, up_ref, down_ref)
    finals = (gate_out, up_out, down_out)
    for which in range(3):
        low[0, 0, which, own_rows] = weights[which][...].astype(jnp.bfloat16)
    scale(0)
    pl.semaphore_wait(barrier, heads + groups - 2)
    send_tokens(0, 0)
    send_tokens(0, 1)
    for which in range(3):
        send_low(0, which)
    for span in range(spans):
        send_queries(span)
    for span in range(1, spans):
        scale(span)
    for span in range(spans):
        for kind in range(2):
            own_tokens(span, kind)
        tok_query[span, member] = q_ref[span, :, columns(quest)]

    for span in range(spans):
        for which in range(3):
            for step in range(1, groups):
                source = within(step)
                low_copy(span, which, source, source).wait_recv()
            if span > 0:
                chain_start(span, which)
        if span > 0:
            send_att(span - 1)

        def forward(step, carry):
            slot = lax.rem(head + step, heads)

            @pl.when(step > 0)
            def _():
                wait_tokens(span, 0, slot)
                wait_tokens(span, 1, slot)

            keys = tok[span, 0, slot]
            first = mm(keys, low[span, 0, 0], 1, 1)
            second = mm(keys, low[span, 0, 1], 1, 1)
            back = mm(tok[span, 1, slot], low[span, 0, 2], 1, 0)
            sig = sigmoid(first)
            silu_first = first * sig
            slope = sig * (1.0 + first * (1.0 - sig))
            acts[slot] = (silu_first * second).astype(jnp.bfloat16)
            d_gate[slot] = (back * second * slope).astype(jnp.bfloat16)
            d_up[slot] = (back * silu_first).astype(jnp.bfloat16)
            return carry

        lax.fori_loop(0, heads, forward, 0)
        if span == 0:
            for which in range(3):
                chain_start(span, which)
        keys = tok[span, 0].reshape(heads * count, width)
        scaled = tok[span, 1].reshape(heads * count, width)
        pairs = (
            (d_gate[...].reshape(heads * count, -1), keys),
            (d_up[...].reshape(heads * count, -1), keys),
            (scaled, acts[...].reshape(heads * count, -1)),
        )
        for which in range(3):
            product = mm(pairs[which][0], pairs[which][1], 0, 0)
            grad[which] = product
            low_grad[span, which] = product.astype(jnp.bfloat16)
            for step in range(1, groups):
                target = within(step)
                grad_copy(span, which, member, target).start()

        for which in range(3):
            chain_pass(span, which)
        if span + 1 < spans:
            for kind in range(2):
                send_tokens(span + 1, kind)

        def answer(step, carry):
            slot = lax.rem(member + step, groups)

            @pl.when(step > 0)
            def _():
                query_copy(span, head, slot, slot).wait_recv()

            queries = tok_query[span, slot]
            first = mm(queries, low[span, held, 0], 1, 1)
            second = mm(queries, low[span, held, 1], 1, 1)
            hidden = (first * sigmoid(first) * second).astype(jnp.bfloat16)
            out_buf[span, slot] = mm(hidden, low[span, held, 2], 1, 1).astype(jnp.bfloat16)
            if span == spans - 1:

                @pl.when(step > 0)
                def _():
                    att_copy(span, slot, quest, member, slot).start()

            return carry

        def collect():
            for which in range(3):
                summed = grad[which, own_rows]
                for step in range(1, groups):
                    source = within(step)
                    grad_copy(span, which, source, source).wait_recv()
                    summed = summed + grad_in[span, which, source].astype(jnp.float32)
                total[which] = summed
                squared = summed * summed
                by_row = jnp.sum(squared.reshape(rows // 8, 8, width), axis=0)
                lanes = by_row[:, :128]
                for at in range(128, width, 128):
                    lanes = lanes + by_row[:, at : at + 128]
                square[span, which] = lanes
            for step in range(1, groups):
                square_copy(span, member, within(step)).start()

        def refresh():
            for step in range(1, groups):
                source = within(step)
                square_copy(span, source, source).wait_recv()
            for which in range(3):
                sums = square[span, which]
                for step in range(1, groups):
                    sums = sums + square_in[span, within(step), which]
                block_mean = jnp.sum(sums, keepdims=True) / (rows * groups * width)
                factor = lax.rsqrt(block_mean + 1e-06) / math.sqrt(width)
                before = weights[which][...] if span == 0 else master[which]
                stepped = before + total[which] * factor
                row_mean = jnp.mean(stepped * stepped, axis=1, keepdims=True)
                after = stepped * (lax.rsqrt(row_mean + 1e-06) / math.sqrt(width))
                if span == spans - 1:
                    finals[which][...] = after
                else:
                    master[which] = after
                    low[span + 1, 0, which, own_rows] = after.astype(jnp.bfloat16)
                    send_low(span + 1, which)

        collect()
        if span + 1 < spans:
            refresh()
        lax.fori_loop(0, groups, answer, 0)
        att_ref[span, :, columns(quest)] = out_buf[span, member]
        if span + 1 == spans:
            refresh()

    for span in range(spans):
        for step in range(1, heads):
            other = across(step)
            for kind in range(2):
                token_copy(span, kind, other, other, other).wait_send()
        for which in range(3):
            chain_finish(span, which)
        for step in range(1, groups):
            other = within(step)
            att_copy(span, other, query_head(other), other, other).wait_recv()
            att_copy(span, other, quest, member, other).wait_send()
            query_copy(span, query_head(other), member, other).wait_send()
        for step in range(1, groups):
            other = within(step)
            for which in range(3):
                low_copy(span, which, other, other).wait_send()
                grad_copy(span, which, other, other).wait_send()
            square_copy(span, other, other).wait_send()


def per_device_fused(
    heads, groups, query_rows, key_rows, value_rows, step_rates, gate_weight, up_weight, down_weight
):
    spans, count, full = query_rows.shape
    rows, width = gate_weight.shape
    block = rows * groups
    low = jnp.bfloat16
    vmem = pl.BlockSpec(memory_space=pltpu.VMEM)
    weight = jax.ShapeDtypeStruct((rows, width), jnp.float32)
    dma = pltpu.SemaphoreType.DMA
    return pl.pallas_call(
        functools.partial(fused_kernel, heads, groups),
        out_shape=(
            jax.ShapeDtypeStruct((spans, count, full), low),
            weight,
            weight,
            weight,
        ),
        in_specs=[vmem] * 7,
        out_specs=(vmem,) * 4,
        scratch_shapes=[
            pltpu.VMEM((spans, count, full), low),
            pltpu.VMEM((spans, 2, heads, count, width), low),
            pltpu.VMEM((spans, groups, count, width), low),
            pltpu.VMEM((spans, groups, count, width), low),
            pltpu.VMEM((spans, 2, 3, block, width), low),
            pltpu.VMEM((spans, 3, block, width), low),
            pltpu.VMEM((3, block, width), jnp.float32),
            pltpu.VMEM((spans, 3, groups, rows, width), low),
            pltpu.VMEM((3, rows, width), jnp.float32),
            pltpu.VMEM((3, rows, width), jnp.float32),
            pltpu.VMEM((heads, count, width), low),
            pltpu.VMEM((heads, count, width), low),
            pltpu.VMEM((heads, count, width), low),
            pltpu.VMEM((spans, 3, 8, 128), jnp.float32),
            pltpu.VMEM((spans, groups, 3, 8, 128), jnp.float32),
            dma((spans, 2, heads)),
            dma((spans, 2, heads)),
            dma((spans, groups)),
            dma((spans, groups)),
            dma((spans, groups)),
            dma((spans, groups)),
            dma((spans, 3, PIECES, 2)),
            dma((spans, 3, PIECES)),
            dma((spans, 3, groups)),
            dma((spans, 3, groups)),
            dma((spans, 3, groups)),
            dma((spans, 3, groups)),
            dma((spans, groups)),
            dma((spans, groups)),
        ],
        compiler_params=pltpu.CompilerParams(
            collective_id=0, has_side_effects=True, vmem_limit_bytes=40 * 2**20
        ),
    )(query_rows, key_rows, value_rows, step_rates, gate_weight, up_weight, down_weight)


def per_device(query_rows, key_rows, value_rows, step_rates, gate_weight, up_weight, down_weight):
    arguments = (
        query_rows, key_rows, value_rows, step_rates, gate_weight, up_weight, down_weight
    )
    heads = step_rates.shape[2]
    size = lax.axis_size("ctx")
    rows, width = gate_weight.shape
    count = query_rows.shape[1]
    groups = size // heads
    fits = (
        size % heads == 0
        and down_weight.shape == gate_weight.shape
        and rows * groups == width
        and query_rows.shape[2] == heads * width
        and rows % 16 == 0
        and width % 128 == 0
        and count % 16 == 0
        and groups == heads
        and heads % 2 == 0
        and width % (16 * PIECES) == 0
    )
    if fits:
        return per_device_fused(heads, groups, *arguments)
    return per_device_general(*arguments)


def solution(mesh):
    placed = (
        P(None, ("parts", "ctx"), None),
        P(None, ("parts", "ctx"), None),
        P(None, ("parts", "ctx"), None),
        P(None, ("parts", "ctx"), None),
        P(("parts", "ctx"), None),
        P(("parts", "ctx"), None),
        P(("parts", "ctx"), None),
    )
    return jax.shard_map(
        per_device,
        mesh=mesh,
        in_specs=placed,
        out_specs=(
            P(None, ("parts", "ctx"), None),
            P(("parts", "ctx"), None),
            P(("parts", "ctx"), None),
            P(("parts", "ctx"), None),
        ),
        check_vma=False,
    )
```

```python
import functools
import math

import jax
import jax.numpy as jnp
from jax import lax
from jax.experimental import pallas as pl
from jax.experimental.pallas import tpu as pltpu
from jax.sharding import PartitionSpec as P


def from_partner(value, axis, apart):
    mask = 2**apart
    pairs = [(source, source ^ mask) for source in range(lax.axis_size(axis))]
    return lax.ppermute(value, axis, pairs)


def silu_parts(values):
    sig = jax.nn.sigmoid(values)
    return (values * sig, sig * (1.0 + values * (1.0 - sig)))


def span_pass(queries, keys_here, scaled_rows, gate_low, up_low, down_low, heads):
    count = queries.shape[0]
    width = gate_low.shape[1]
    hidden = gate_low.shape[0] // heads
    gate_three = gate_low.reshape(heads, hidden, width)
    up_three = up_low.reshape(heads, hidden, width)
    down_three = down_low.reshape(heads, width, hidden)
    key_three = keys_here.reshape(count, heads, width)
    first = jnp.einsum("thd,hfd->thf", key_three, gate_three, preferred_element_type=jnp.float32)
    second = jnp.einsum("thd,hfd->thf", key_three, up_three, preferred_element_type=jnp.float32)
    silu_first, slope = silu_parts(first)
    acts = (silu_first * second).astype(jnp.bfloat16)
    scaled = scaled_rows.reshape(count, heads, width)
    back = jnp.einsum("thd,hdf->thf", scaled, down_three, preferred_element_type=jnp.float32)
    d_gate = (back * second * slope).astype(jnp.bfloat16)
    d_up = (back * silu_first).astype(jnp.bfloat16)
    grad_gate = jnp.einsum(
        "thf,thd->hfd", d_gate, key_three, preferred_element_type=jnp.float32
    ).reshape(heads * hidden, width)
    grad_up = jnp.einsum(
        "thf,thd->hfd", d_up, key_three, preferred_element_type=jnp.float32
    ).reshape(heads * hidden, width)
    grad_down = jnp.einsum(
        "thd,thf->hdf", scaled, acts, preferred_element_type=jnp.float32
    ).reshape(heads * width, hidden)
    query_three = queries.reshape(count, heads, width)
    query_gate = jnp.einsum(
        "thd,hfd->thf", query_three, gate_three, preferred_element_type=jnp.float32
    )
    query_up = jnp.einsum("thd,hfd->thf", query_three, up_three, preferred_element_type=jnp.float32)
    query_acts = (jax.nn.silu(query_gate) * query_up).astype(jnp.bfloat16)
    output = jnp.einsum("thf,hdf->thd", query_acts, down_three, preferred_element_type=jnp.float32)
    return (
        output.reshape(count, heads * width).astype(jnp.bfloat16),
        (grad_gate, grad_up, grad_down),
    )


def head_member(row_count, offset, per_head, heads):
    row_ids = offset + jnp.arange(row_count, dtype=jnp.int32)
    head_ids = jnp.arange(heads, dtype=jnp.int32)
    return (row_ids[:, None] // per_head == head_ids[None, :]).astype(jnp.float32)


def head_partial(gradient, member):
    return jnp.sum(member * jnp.sum(gradient * gradient, axis=1)[:, None], axis=0)


def refresh_rows(matrix, gradient, member, head_total, per_head):
    columns = matrix.shape[1]
    block_mean = head_total / (per_head * columns)
    factor = lax.rsqrt(block_mean + 1e-06) / math.sqrt(columns)
    row_factor = jnp.sum(member * factor[None, :], axis=1)
    stepped = matrix + gradient * row_factor[:, None]
    row_mean = jnp.mean(stepped * stepped, axis=1, keepdims=True)
    return stepped * lax.rsqrt(row_mean + 1e-06) / math.sqrt(columns)


def update_shards(masters, shares, heads):
    row_count = masters[0].shape[0]
    total_rows = row_count * lax.axis_size("ctx")
    per_head = total_rows // heads
    offset = lax.axis_index("ctx") * row_count
    member = head_member(row_count, offset, per_head, heads)
    partials = [head_partial(shares[i], member) for i in range(3)]
    totals = lax.psum((partials[0], partials[1], partials[2]), "ctx")
    return tuple(
        (refresh_rows(masters[i], shares[i], member, totals[i], per_head) for i in range(3))
    )


def scale_values(value_rows, step_rates):
    span_count, count, total_width = value_rows.shape
    heads = step_rates.shape[2]
    spread = value_rows.reshape(span_count, count, heads, total_width // heads).astype(jnp.float32)
    return (
        (step_rates[:, :, :, None] * spread)
        .astype(jnp.bfloat16)
        .reshape(span_count, count, total_width)
    )


def to_heads(array, groups, heads):
    span_count, count, total_width = array.shape
    slab = count // groups
    width = total_width // heads
    spread = array.reshape(span_count, groups, slab, heads, width).transpose(3, 1, 0, 2, 4)
    return spread.reshape(heads * groups, span_count, slab, width)


def from_heads(array, groups, heads):
    devices, span_count, slab, width = array.shape
    spread = array.reshape(heads, groups, span_count, slab, width).transpose(2, 1, 3, 0, 4)
    return spread.reshape(span_count, groups * slab, heads * width)


def per_device_general(query_rows, key_rows, value_rows, step_rates, gate_weight, up_weight, down_weight):
    heads = step_rates.shape[2]
    span_count = query_rows.shape[0]
    scaled_all = scale_values(value_rows, step_rates)
    results = []
    groups = lax.axis_size("ctx") // heads
    bits = groups.bit_length() - 1
    position = lax.axis_index("ctx")
    moved = (
        lax.all_to_all(
            to_heads(query_rows, groups, heads), "ctx", split_axis=0, concat_axis=0, tiled=True
        ),
        lax.all_to_all(
            to_heads(key_rows, groups, heads), "ctx", split_axis=0, concat_axis=0, tiled=True
        ),
        lax.all_to_all(
            to_heads(scaled_all, groups, heads), "ctx", split_axis=0, concat_axis=0, tiled=True
        ),
    )
    width = moved[0].shape[3]
    masters = (gate_weight, up_weight, down_weight)
    for span_index in range(span_count):
        blocks = tuple((matrix.astype(jnp.bfloat16) for matrix in masters))
        for level in range(bits):
            other = from_partner((blocks[0], blocks[1], blocks[2]), "ctx", level)
            upper_side = position >> level & 1 == 1
            blocks = tuple(
                (
                    jnp.where(
                        upper_side,
                        jnp.concatenate([other[i], blocks[i]], axis=0),
                        jnp.concatenate([blocks[i], other[i]], axis=0),
                    )
                    for i in range(3)
                )
            )
        queries = moved[0][:, span_index].reshape(-1, width)
        keys_here = moved[1][:, span_index].reshape(-1, width)
        scaled_rows = moved[2][:, span_index].reshape(-1, width)
        output, grads = span_pass(
            queries, keys_here, scaled_rows, blocks[0], blocks[1], blocks[2], 1
        )
        results.append(output.reshape(moved[0].shape[0], moved[0].shape[2], width))
        for level in reversed(range(bits)):
            upper_side = position >> level & 1 == 1
            halves = [grad.shape[0] // 2 for grad in grads]
            kept = tuple(
                (
                    jnp.where(upper_side, grads[i][halves[i] :], grads[i][: halves[i]])
                    for i in range(3)
                )
            )
            sent = tuple(
                (
                    jnp.where(upper_side, grads[i][: halves[i]], grads[i][halves[i] :])
                    for i in range(3)
                )
            )
            other = from_partner((sent[0], sent[1], sent[2]), "ctx", level)
            grads = tuple((kept[i] + other[i] for i in range(3)))
        masters = update_shards(masters, grads, heads)
    stacked = jnp.stack(results, axis=1)
    returned = lax.all_to_all(stacked, "ctx", split_axis=0, concat_axis=0, tiled=True)
    return (from_heads(returned, groups, heads), masters[0], masters[1], masters[2])


def mm(left, right, left_dim, right_dim):
    return lax.dot_general(
        left,
        right,
        (((left_dim,), (right_dim,)), ((), ())),
        preferred_element_type=jnp.float32,
    )


def sigmoid(values):
    return 0.5 * jnp.tanh(0.5 * values) + 0.5


def fused_kernel(
    heads,
    groups,
    q_ref,
    k_ref,
    v_ref,
    r_ref,
    gate_ref,
    up_ref,
    down_ref,
    att_ref,
    gate_out,
    up_out,
    down_out,
    scaled_buf,
    tok,
    out_buf,
    low,
    low_grad,
    grad,
    mate_in,
    pair_sum,
    grad_in,
    master,
    total,
    d_gate,
    d_up,
    acts,
    square,
    square_in,
    tok_send,
    tok_recv,
    att_send,
    att_recv,
    low_send,
    low_recv,
    mate_send,
    mate_recv,
    grad_send,
    grad_recv,
    square_send,
    square_recv,
):
    spans, count, _ = q_ref.shape
    rows, width = gate_ref.shape
    position = lax.axis_index("ctx")
    head = lax.div(position, groups)
    member = lax.rem(position, groups)

    side = lax.rem(member, 2)
    pair = lax.div(member, 2)
    mate = member + 1 - 2 * side
    pairs_here = groups // 2

    def alike(step):
        return lax.rem(member + 2 * step, groups)

    def across(step):
        return lax.rem(head + step, heads)

    def within(step):
        return lax.rem(member + step, groups)

    def far(which):
        return {"ctx": which * groups + member}

    def near(which):
        return {"ctx": head * groups + which}

    def columns(which):
        return pl.ds(pl.multiple_of(which * width, 128), width)

    def rows_of(which):
        return pl.ds(pl.multiple_of(which * rows, 16), rows)

    own_rows = rows_of(member)
    own_columns = columns(head)

    barrier = pltpu.get_barrier_semaphore()
    for step in range(1, heads):
        pl.semaphore_signal(
            barrier, inc=1, device_id=far(across(step)), device_id_type=pl.DeviceIdType.MESH
        )
    for step in range(1, groups):
        pl.semaphore_signal(
            barrier, inc=1, device_id=near(within(step)), device_id_type=pl.DeviceIdType.MESH
        )

    def scale(span):
        for each in range(heads):
            part = v_ref[span, :, each * width : (each + 1) * width].astype(jnp.float32)
            rate = r_ref[span, :, each : each + 1]
            scaled_buf[span, :, each * width : (each + 1) * width] = (part * rate).astype(
                jnp.bfloat16
            )

    def token_copy(span, kind, source_at, slot, target):
        source = (q_ref, k_ref, scaled_buf)[kind]
        return pltpu.make_async_remote_copy(
            src_ref=source.at[span, :, columns(source_at)],
            dst_ref=tok.at[span, kind, slot],
            send_sem=tok_send.at[span, kind, target],
            recv_sem=tok_recv.at[span, kind, slot],
            device_id=far(target),
            device_id_type=pl.DeviceIdType.MESH,
        )

    def send_tokens(span, kind):
        for step in range(1, heads):
            target = across(step)
            token_copy(span, kind, target, head, target).start()

    def wait_tokens(span, kind, source):
        token_copy(span, kind, source, source, source).wait_recv()

    def own_tokens(span, kind):
        source = (q_ref, k_ref, scaled_buf)[kind]
        tok[span, kind, head] = source[span, :, own_columns]

    def att_copy(span, slot, column, target):
        return pltpu.make_async_remote_copy(
            src_ref=out_buf.at[span, slot],
            dst_ref=att_ref.at[span, :, columns(column)],
            send_sem=att_send.at[span, slot],
            recv_sem=att_recv.at[span, column],
            device_id=far(target),
            device_id_type=pl.DeviceIdType.MESH,
        )

    def low_copy(span, which, block, target, relay):
        return pltpu.make_async_remote_copy(
            src_ref=low.at[span, which, rows_of(block)],
            dst_ref=low.at[span, which, rows_of(block)],
            send_sem=low_send.at[span, which, relay, block if relay else target],
            recv_sem=low_recv.at[span, which, block],
            device_id=near(target),
            device_id_type=pl.DeviceIdType.MESH,
        )

    def mate_copy(span, which):
        return pltpu.make_async_remote_copy(
            src_ref=low_grad.at[span, which, 1 - side],
            dst_ref=mate_in.at[span, which],
            send_sem=mate_send.at[span, which],
            recv_sem=mate_recv.at[span, which],
            device_id=near(mate),
            device_id_type=pl.DeviceIdType.MESH,
        )

    def grad_copy(span, which, slot, target):
        return pltpu.make_async_remote_copy(
            src_ref=pair_sum.at[span, which, target],
            dst_ref=grad_in.at[span, which, slot],
            send_sem=grad_send.at[span, which, target],
            recv_sem=grad_recv.at[span, which, slot],
            device_id=near(2 * target + side),
            device_id_type=pl.DeviceIdType.MESH,
        )

    def square_copy(span, slot, target):
        return pltpu.make_async_remote_copy(
            src_ref=square.at[span],
            dst_ref=square_in.at[span, slot],
            send_sem=square_send.at[span, target],
            recv_sem=square_recv.at[span, slot],
            device_id=near(target),
            device_id_type=pl.DeviceIdType.MESH,
        )

    def send_low(span, which):
        for step in range(1, pairs_here):
            low_copy(span, which, member, alike(step), 0).start()
        low_copy(span, which, member, mate, 0).start()

    def gather_low(span):
        for which in range(3):
            for step in range(1, pairs_here):
                other = alike(step)
                low_copy(span, which, other, other, 0).wait_recv()
                low_copy(span, which, other, mate, 1).start()

    def finish_low(span):
        for which in range(3):
            low_copy(span, which, mate, mate, 0).wait_recv()
            for step in range(1, pairs_here):
                other = alike(step) + mate - member
                low_copy(span, which, other, mate, 1).wait_recv()

    weights = (gate_ref, up_ref, down_ref)
    finals = (gate_out, up_out, down_out)
    for which in range(3):
        low[0, which, own_rows] = weights[which][...].astype(jnp.bfloat16)
    scale(0)
    pl.semaphore_wait(barrier, heads + groups - 2)
    send_tokens(0, 1)
    send_tokens(0, 2)
    for which in range(3):
        send_low(0, which)
    for span in range(1, spans):
        scale(span)
    for span in range(spans):
        for kind in range(3):
            own_tokens(span, kind)
    for span in range(spans):
        gather_low(span)
        finish_low(span)

        def forward(step, carry):
            duo = lax.rem(lax.div(head, 2) + step, heads // 2)
            for at in range(2):
                slot = 2 * duo + at

                @pl.when(slot != head)
                def _():
                    wait_tokens(span, 1, slot)
                    wait_tokens(span, 2, slot)

            if span == 0:

                @pl.when(step == heads // 2 - 1)
                def _():
                    for later in range(1, spans):
                        send_tokens(later, 1)
                        send_tokens(later, 2)
                    for later in range(spans):
                        send_tokens(later, 0)

            keys = tok[span, 1, pl.ds(2 * duo, 2)].reshape(2 * count, width)
            first = mm(keys, low[span, 0], 1, 1)
            second = mm(keys, low[span, 1], 1, 1)
            sent = tok[span, 2, pl.ds(2 * duo, 2)].reshape(2 * count, width)
            back = mm(sent, low[span, 2], 1, 0)
            sig = sigmoid(first)
            silu_first = first * sig
            slope = sig * (1.0 + first * (1.0 - sig))
            acts[duo] = (silu_first * second).astype(jnp.bfloat16)
            d_gate[duo] = (back * second * slope).astype(jnp.bfloat16)
            d_up[duo] = (back * silu_first).astype(jnp.bfloat16)
            return carry

        lax.fori_loop(0, heads // 2, forward, 0)
        keys = tok[span, 1].reshape(heads * count, width)
        scaled = tok[span, 2].reshape(heads * count, width)
        pairs = (
            (d_gate[...].reshape(heads * count, -1), keys),
            (d_up[...].reshape(heads * count, -1), keys),
            (scaled, acts[...].reshape(heads * count, -1)),
        )
        for which in range(3):
            product = mm(pairs[which][0], pairs[which][1], 0, 0)
            grad[which] = product
            lowered = product.astype(jnp.bfloat16)
            for each in range(groups):
                low_grad[span, which, each % 2, each // 2] = lowered[
                    each * rows : (each + 1) * rows
                ]
            mate_copy(span, which).start()
        for which in range(3):
            mate_copy(span, which).wait_recv()
            for step in range(1, pairs_here):
                other = lax.div(alike(step), 2)
                pair_sum[span, which, other] = (
                    grad[which, rows_of(alike(step))]
                    + mate_in[span, which, other].astype(jnp.float32)
                ).astype(jnp.bfloat16)
                grad_copy(span, which, pair, other).start()

        def answer(step, carry):
            duo = lax.rem(lax.div(head, 2) + step, heads // 2)
            for at in range(2):
                slot = 2 * duo + at

                @pl.when(slot != head)
                def _():
                    wait_tokens(span, 0, slot)

            queries = tok[span, 0, pl.ds(2 * duo, 2)].reshape(2 * count, width)
            first = mm(queries, low[span, 0], 1, 1)
            second = mm(queries, low[span, 1], 1, 1)
            hidden = (first * sigmoid(first) * second).astype(jnp.bfloat16)
            answers = mm(hidden, low[span, 2], 1, 1).astype(jnp.bfloat16)
            for at in range(2):
                slot = 2 * duo + at
                out_buf[span, slot] = answers[at * count : (at + 1) * count]

                @pl.when(slot != head)
                def _():
                    att_copy(span, slot, head, slot).start()

            return carry

        def collect():
            for which in range(3):
                summed = grad[which, own_rows] + mate_in[span, which, pair].astype(jnp.float32)
                for step in range(1, pairs_here):
                    source = lax.div(alike(step), 2)
                    grad_copy(span, which, source, source).wait_recv()
                    summed = summed + grad_in[span, which, source].astype(jnp.float32)
                total[which] = summed
                squared = summed * summed
                by_row = jnp.sum(squared.reshape(rows // 8, 8, width), axis=0)
                lanes = by_row[:, :128]
                for at in range(128, width, 128):
                    lanes = lanes + by_row[:, at : at + 128]
                square[span, which] = lanes
            for step in range(1, groups):
                square_copy(span, member, within(step)).start()

        def refresh():
            for step in range(1, groups):
                source = within(step)
                square_copy(span, source, source).wait_recv()
            for which in range(3):
                sums = square[span, which]
                for step in range(1, groups):
                    sums = sums + square_in[span, within(step), which]
                block_mean = jnp.sum(sums, keepdims=True) / (rows * groups * width)
                factor = lax.rsqrt(block_mean + 1e-06) / math.sqrt(width)
                before = weights[which][...] if span == 0 else master[which]
                stepped = before + total[which] * factor
                row_mean = jnp.mean(stepped * stepped, axis=1, keepdims=True)
                after = stepped * (lax.rsqrt(row_mean + 1e-06) / math.sqrt(width))
                if span == spans - 1:
                    finals[which][...] = after
                else:
                    master[which] = after
                    low[span + 1, which, own_rows] = after.astype(jnp.bfloat16)
                    send_low(span + 1, which)

        if span + 1 < spans:
            collect()
            refresh()
        lax.fori_loop(0, heads // 2, answer, 0)
        if span + 1 == spans:
            collect()
            refresh()
        att_ref[span, :, own_columns] = out_buf[span, head]

    for span in range(spans):
        for step in range(1, heads):
            other = across(step)
            att_copy(span, other, other, other).wait_recv()
            att_copy(span, other, other, other).wait_send()
            for kind in range(3):
                token_copy(span, kind, other, other, other).wait_send()
        for step in range(1, groups):
            other = within(step)
            square_copy(span, other, other).wait_send()
        for which in range(3):
            mate_copy(span, which).wait_send()
            low_copy(span, which, member, mate, 0).wait_send()
            for step in range(1, pairs_here):
                other = alike(step)
                low_copy(span, which, member, other, 0).wait_send()
                low_copy(span, which, other, mate, 1).wait_send()
                grad_copy(span, which, pair, lax.div(other, 2)).wait_send()


def per_device_fused(
    heads, groups, query_rows, key_rows, value_rows, step_rates, gate_weight, up_weight, down_weight
):
    spans, count, full = query_rows.shape
    rows, width = gate_weight.shape
    block = rows * groups
    low = jnp.bfloat16
    vmem = pl.BlockSpec(memory_space=pltpu.VMEM)
    weight = jax.ShapeDtypeStruct((rows, width), jnp.float32)
    dma = pltpu.SemaphoreType.DMA
    return pl.pallas_call(
        functools.partial(fused_kernel, heads, groups),
        out_shape=(
            jax.ShapeDtypeStruct((spans, count, full), low),
            weight,
            weight,
            weight,
        ),
        in_specs=[vmem] * 7,
        out_specs=(vmem,) * 4,
        scratch_shapes=[
            pltpu.VMEM((spans, count, full), low),
            pltpu.VMEM((spans, 3, heads, count, width), low),
            pltpu.VMEM((spans, heads, count, width), low),
            pltpu.VMEM((spans, 3, block, width), low),
            pltpu.VMEM((spans, 3, 2, groups // 2, rows, width), low),
            pltpu.VMEM((3, block, width), jnp.float32),
            pltpu.VMEM((spans, 3, groups // 2, rows, width), low),
            pltpu.VMEM((spans, 3, groups // 2, rows, width), low),
            pltpu.VMEM((spans, 3, groups // 2, rows, width), low),
            pltpu.VMEM((3, rows, width), jnp.float32),
            pltpu.VMEM((3, rows, width), jnp.float32),
            pltpu.VMEM((heads // 2, 2 * count, width), low),
            pltpu.VMEM((heads // 2, 2 * count, width), low),
            pltpu.VMEM((heads // 2, 2 * count, width), low),
            pltpu.VMEM((spans, 3, 8, 128), jnp.float32),
            pltpu.VMEM((spans, groups, 3, 8, 128), jnp.float32),
            dma((spans, 3, heads)),
            dma((spans, 3, heads)),
            dma((spans, heads)),
            dma((spans, heads)),
            dma((spans, 3, 2, groups)),
            dma((spans, 3, groups)),
            dma((spans, 3)),
            dma((spans, 3)),
            dma((spans, 3, groups // 2)),
            dma((spans, 3, groups // 2)),
            dma((spans, groups)),
            dma((spans, groups)),
        ],
        compiler_params=pltpu.CompilerParams(
            collective_id=0, has_side_effects=True, vmem_limit_bytes=40 * 2**20
        ),
    )(query_rows, key_rows, value_rows, step_rates, gate_weight, up_weight, down_weight)


def per_device(query_rows, key_rows, value_rows, step_rates, gate_weight, up_weight, down_weight):
    arguments = (
        query_rows, key_rows, value_rows, step_rates, gate_weight, up_weight, down_weight
    )
    heads = step_rates.shape[2]
    size = lax.axis_size("ctx")
    rows, width = gate_weight.shape
    count = query_rows.shape[1]
    groups = size // heads
    fits = (
        size % heads == 0
        and down_weight.shape == gate_weight.shape
        and rows * groups == width
        and query_rows.shape[2] == heads * width
        and rows % 16 == 0
        and width % 128 == 0
        and count % 16 == 0
        and heads % 2 == 0
        and groups in (2, 4, 6, 8)
    )
    if fits:
        return per_device_fused(heads, groups, *arguments)
    return per_device_general(*arguments)


def solution(mesh):
    placed = (
        P(None, ("parts", "ctx"), None),
        P(None, ("parts", "ctx"), None),
        P(None, ("parts", "ctx"), None),
        P(None, ("parts", "ctx"), None),
        P(("parts", "ctx"), None),
        P(("parts", "ctx"), None),
        P(("parts", "ctx"), None),
    )
    return jax.shard_map(
        per_device,
        mesh=mesh,
        in_specs=placed,
        out_specs=(
            P(None, ("parts", "ctx"), None),
            P(("parts", "ctx"), None),
            P(("parts", "ctx"), None),
            P(("parts", "ctx"), None),
        ),
        check_vma=False,
    )
```
